32 devices in a mesh: groups: 2 (over y), expert: 8 (over z, x), mp: 2 (over core).
Axes of the slice: x: 2, y: 2, z: 4, core: 2. Of those that a mesh axis runs over, the one named last changes fastest.
Arguments:
- tokens: bfloat16 [1024, 6144], P(('groups', 'expert'), 'mp'), parts along dimension 0, may hold values from -6 to 6
- expert_ids: int32 [1024, 2], P(('groups', 'expert')), parts along dimension 0, may hold values from 0 to 7, all different within a row; in each aligned block of 64 rows (0 to 63, 64 to 127, ...) at most 24 rows name the same one
- gate_ranks: int32 [1024, 2], P(('groups', 'expert')), parts along dimension 0, may hold values from 1 to 256
- limits: int32 [16, 8], P(('groups', 'expert')), parts along dimension 0, may hold values from 12 to 24
- w_in: bfloat16 [8, 6144, 2, 4096], P('expert', None, None, 'mp'), may hold values from -0.078125 to 0.078125
- w_out: bfloat16 [8, 4096, 6144], P('expert', 'mp'), may hold values from -0.0625 to 0.0625
Outputs:
- mixed: bfloat16 [1024, 6144], P(('groups', 'expert'), 'mp'), parts along dimension 0
The draws below stay inside these ranges and needn't reach their ends.
There are 2 independent parts, one for each index of `groups`. The reference program is written for one: setup_inputs(seed, part) draws one part's arguments, and reference() takes and returns one part's arrays. A program takes and returns all parts, laid end to end along the dimension named above; an argument that names none is the same for every part. Nothing has to cross between parts.
Inputs may be any that keep to these rules, and one draw needn't show every extreme that they name: `expert_ids`: within one block of 64 rows (the tokens of one index of expert) no expert is named by more than 24 picks; the two picks of a token differ.
All inputs are finite; a program needn't handle non-finite values.
Results may differ from the reference program's by a relative error of at most 0.0058.
Values may be sent and summed in bfloat16 or wider, within the bound.
A program may use at most 320 MiB of HBM per device.

```python
import math
import jax
import jax.numpy as jnp
import numpy as np
from jax import lax

D = 6144
NUM_EXPERTS = 8
FF_WIN = 8192
EXP_WIN = 4
TOK_DEV = 64
CAP = 24
SLICES = 2
SLICE_W = 4096
TOKENS = 512
N_EXPERT = 8


def place_ends(array, stream_key, low, largest):
    extent = array.shape
    spot = [jax.random.randint(jax.random.fold_in(stream_key, axis), (), 0, extent[axis]) for axis in range(len(extent))]
    array = array.at[tuple(spot)].set(low)
    longest = extent.index(max(extent))
    spot[longest] = (spot[longest] + 1) % extent[longest]
    return array.at[tuple(spot)].set(largest)


def steps_of(own_key, dims, split, smallest, high):
    loudness = 1.0
    for dim, shards_of in split:
        draws = jax.random.uniform(jax.random.fold_in(jax.random.fold_in(own_key, 6), dim), (shards_of,), jnp.float32, smallest / len(split), high / len(split))
        loudness = loudness * jnp.repeat(jnp.exp(draws), dims[dim] // shards_of).reshape((-1,) + (1,) * (len(dims) - 1 - dim))
    return loudness


def deal_out(own_key, own, number, rows, amount, top, limit, lean):
    order = jax.random.permutation(own_key, amount)
    packed, usual = shares(amount, rows * top, limit, lean, True), shares(amount, rows * top, limit, lean, False)
    places = jnp.arange(amount)

    def named(tallies, turn):
        used = int((tallies > 0).sum())
        fixed = max(1, used // 4)
        passed = fixed + (places - fixed + turn * (used - fixed)) % max(1, amount - fixed)
        return jnp.zeros((amount,), jnp.int32).at[order[jnp.where(places < fixed, places, passed)]].set(jnp.asarray(tallies, jnp.int32))

    tallies = jnp.where(number % 4 == 0, named(packed, number // 4), named(usual, number - number // 4 - 1))
    mixed = jax.random.permutation(jax.random.fold_in(own, 3), amount)
    donor, sink = mixed[0:amount // 2 * 2:2], mixed[1:amount // 2 * 2:2]
    room = jnp.minimum(tallies[donor] - 1, limit - tallies[sink]) // 2
    room = jnp.where((donor == order[0]) | (sink == order[0]) | (tallies[sink] == 0), 0, jnp.maximum(room, 0))
    passed = jax.random.randint(jax.random.fold_in(own, 4), (amount // 2,), 0, 1 << 20) % (room + 1)
    tallies = tallies.at[donor].add(-passed).at[sink].add(passed)
    items = jnp.searchsorted(jnp.cumsum(tallies), jnp.arange(rows * top), side="right").astype(jnp.int32)
    listing = items.reshape(top, rows).T
    listing = listing[jax.random.permutation(jax.random.fold_in(own, 1), rows)]
    turn = jax.random.randint(jax.random.fold_in(own, 2), (rows, 1), 0, top)
    return jnp.take_along_axis(listing, (jnp.arange(top)[None, :] + turn) % top, axis=1)


def shares(count, total, reach, lean, full):
    loads = [(1 << 20) // math.isqrt(rank ** lean) + 1 for rank in range(1, count + 1)]
    largest = reach if full else min(reach, max(-(-total // count), total * loads[0] // sum(loads)))
    least = 1 if total - largest >= count - 1 else 0
    counts, spare = [largest] + [least] * (count - 1), total - largest - least * (count - 1)
    while spare > 0:
        free = [i for i in range(1, count) if counts[i] < largest] or [i for i in range(1, count) if counts[i] < reach]
        pool, budget = sum([loads[i] for i in free]), spare
        for i in free:
            more = min(reach - counts[i], max(1, budget * loads[i] // pool), spare)
            counts[i] = counts[i] + more
            spare = spare - more
    return np.array(counts)


def centred(stream_key, shape, scale, limit, cuts=(), kind=jnp.bfloat16):
    values = scale * jax.random.normal(stream_key, shape, jnp.float32)
    if cuts:
        values = values * steps_of(stream_key, shape, cuts, -0.22, 0.18)
    return jnp.clip(values, -limit, limit).astype(kind)


def setup_inputs(seed: int = 0, part: int = 0) -> dict:
    key_of = jax.random.split(jax.random.key(seed), 7)
    part_splits = jax.random.split(jax.random.fold_in(key_of[6], part), 7)
    tokens = centred(part_splits[0], (TOKENS, D), 1.0, 6.0, ((0, 8), (1, 2)))
    expert_ids_keys = jax.random.split(jax.random.fold_in(part_splits[1], 1), TOKENS // TOK_DEV)
    expert_ids_turns = jax.random.permutation(jax.random.fold_in(part_splits[1], 3), TOKENS // TOK_DEV)
    expert_ids = jax.vmap(lambda own, number: deal_out(jax.random.fold_in(part_splits[1], 2), own, number, TOK_DEV, NUM_EXPERTS, 2, CAP, 2))(expert_ids_keys, expert_ids_turns).reshape((TOKENS, 2))
    gate_ranks = place_ends(jax.random.randint(part_splits[2], (TOKENS, 2), 1, 257), jax.random.fold_in(part_splits[2], 1), 1, 256).astype(jnp.int32)
    limits = place_ends(jax.random.randint(part_splits[3], (N_EXPERT, NUM_EXPERTS), CAP // 2, CAP + 1), jax.random.fold_in(part_splits[3], 1), CAP // 2, CAP).astype(jnp.int32)
    w_in = centred(key_of[4], (N_EXPERT, D, 2, SLICE_W), D ** -0.5, 0.078125, ((0, 8), (3, 2)))
    w_out = centred(key_of[5], (N_EXPERT, SLICE_W, D), FF_WIN ** -0.5, 0.0625, ((0, 8), (1, 2)))
    return dict(tokens=tokens, expert_ids=expert_ids, gate_ranks=gate_ranks, limits=limits, w_in=w_in, w_out=w_out)


def reference(tokens, expert_ids, gate_ranks, limits, w_in, w_out):
    chosen = expert_ids.reshape(N_EXPERT, TOK_DEV * 2)
    labels = jnp.arange(NUM_EXPERTS, dtype=jnp.int32)
    onehot = (chosen[:, :, None] == labels[None, None, :]).astype(jnp.int32)
    before = jnp.cumsum(onehot, axis=1) - onehot
    position = jnp.sum(before * onehot, axis=2)
    limit_of = jnp.take_along_axis(limits, chosen, axis=1)
    keep_mask = (chosen < EXP_WIN) & (position < limit_of)
    rank_vals = gate_ranks.astype(jnp.float32)
    gate_share = (rank_vals / jnp.sum(rank_vals, axis=1, keepdims=True)).reshape(N_EXPERT, TOK_DEV * 2)
    slot_index = jnp.where(keep_mask, chosen * CAP + position, 0).astype(jnp.int32)
    device_row = jnp.broadcast_to(jnp.arange(N_EXPERT, dtype=jnp.int32)[:, None], chosen.shape)
    token_row = jnp.broadcast_to((jnp.arange(TOK_DEV * 2, dtype=jnp.int32) // 2)[None, :], chosen.shape)
    total_slots = N_EXPERT * EXP_WIN * CAP
    target = jnp.where(keep_mask, device_row * (EXP_WIN * CAP) + slot_index, total_slots).astype(jnp.int32)
    source_of = jnp.full((total_slots,), -1, jnp.int32).at[target.reshape(-1)].set(
        (device_row * TOK_DEV + token_row).reshape(-1).astype(jnp.int32), mode="drop")
    filled = source_of >= 0
    gathered = jnp.where(filled[:, None], tokens[jnp.maximum(source_of, 0)], jnp.zeros((), tokens.dtype))
    gathered = gathered.reshape(N_EXPERT, EXP_WIN, CAP, D)
    results = []
    for expert in range(EXP_WIN):
        flat_rows = gathered[:, expert].reshape(N_EXPERT * CAP, D).astype(jnp.float32)
        block_in = w_in[expert * SLICES:(expert + 1) * SLICES].astype(jnp.float32)
        gate = jnp.einsum("rd,sdh->rsh", flat_rows, block_in[:, :, 0, :], precision=lax.Precision.HIGHEST)
        upper = jnp.einsum("rd,sdh->rsh", flat_rows, block_in[:, :, 1, :], precision=lax.Precision.HIGHEST)
        hidden = (jax.nn.silu(gate) * upper).astype(jnp.bfloat16)
        hidden = lax.optimization_barrier(hidden).astype(jnp.float32)
        block_out = w_out[expert * SLICES:(expert + 1) * SLICES].astype(jnp.float32)
        partial_value = jnp.einsum("rsh,shd->srd", hidden, block_out, precision=lax.Precision.HIGHEST)
        partial_value = lax.optimization_barrier(partial_value.astype(jnp.bfloat16)).astype(jnp.float32)
        results.append(jnp.sum(partial_value, axis=0).reshape(N_EXPERT, CAP, D))
    expert_out = jnp.stack(results, axis=1).reshape(N_EXPERT, EXP_WIN * CAP, D)
    combine = jnp.zeros((N_EXPERT, TOK_DEV, EXP_WIN * CAP), jnp.float32).at[device_row, token_row, slot_index].add(
        jnp.where(keep_mask, gate_share, jnp.zeros((), gate_share.dtype)))
    mixed = jnp.einsum("dtb,dbf->dtf", combine, expert_out, precision=lax.Precision.HIGHEST)
    return mixed.reshape(N_EXPERT * TOK_DEV, D).astype(jnp.bfloat16)
```

```python
import functools
import jax
import jax.numpy as jnp
from jax import lax
from jax.experimental import pallas as pl
from jax.experimental.pallas import tpu as pltpu
from jax.sharding import PartitionSpec as P

D = 6144
NUM_EXPERTS = 8
EXP_WIN = 4
CAP = 24

CHUNKS = 1
STEP = 512
COLS = 512


def gate_up_body(steps, first, last, *refs):
    if first:
        x_ref, w_ref, o_ref, *rest = refs
    else:
        x_ref, w_ref, before_ref, o_ref, *rest = refs
    sums = rest[0] if last else o_ref
    step = pl.program_id(0)

    @pl.when(step == 0)
    def _():
        sums[...] = jnp.zeros_like(sums) if first else before_ref[...]

    depth = w_ref.shape[0]
    rows = x_ref.shape[0] * x_ref.shape[1]
    x = x_ref[...].reshape(rows, depth)
    w = w_ref[...].reshape(depth, sums.shape[1])
    sums[...] += jnp.dot(x, w, preferred_element_type=jnp.float32)

    if last:
        @pl.when(step == steps - 1)
        def _():
            for j in range(o_ref.shape[1] // 128):
                gate = sums[:, 256 * j:256 * j + 128]
                up = sums[:, 256 * j + 128:256 * j + 256]
                o_ref[:, 128 * j:128 * j + 128] = (gate * jax.nn.sigmoid(gate) * up).astype(o_ref.dtype)


def gate_up(x, w, before, chunk, last):
    ranks, halves, depth, width = x.shape
    rows = ranks * depth
    wide = w.shape[1] * 128
    per_half = width // STEP
    half = w.shape[0] // halves // STEP
    steps = halves * per_half
    first = before is None
    in_specs = [
        pl.BlockSpec((ranks, None, depth, STEP), lambda k: (0, k // per_half, 0, k % per_half)),
        pl.BlockSpec((STEP, w.shape[1], 128),
                     lambda k: (k // per_half * half + chunk * per_half + k % per_half, 0, 0)),
    ]
    if not first:
        in_specs.append(pl.BlockSpec((rows, wide), lambda k: (0, 0)))
    out = jax.ShapeDtypeStruct((rows, wide // 2), jnp.bfloat16) if last else jax.ShapeDtypeStruct((rows, wide), jnp.float32)
    return pl.pallas_call(
        functools.partial(gate_up_body, steps, first, last),
        grid=(steps,),
        in_specs=in_specs,
        out_specs=pl.BlockSpec(out.shape, lambda k: (0, 0)),
        out_shape=out,
        scratch_shapes=[pltpu.VMEM((rows, wide), jnp.float32)] if last else [],
        compiler_params=pltpu.CompilerParams(vmem_limit_bytes=48 * 2**20),
        cost_estimate=pl.CostEstimate(flops=2 * rows * halves * width * wide, bytes_accessed=halves * width * wide * 2, transcendentals=0),
    )(*([x, w] if first else [x, w, before]))


def down_body(at_ref, h_ref, w_ref, o_ref):
    o_ref[...] = jnp.dot(h_ref[...], w_ref[...], preferred_element_type=jnp.float32).astype(o_ref.dtype)


def down(hidden, w, at, width, kind):
    rows, depth = hidden.shape
    return pl.pallas_call(
        down_body,
        grid_spec=pltpu.PrefetchScalarGridSpec(
            num_scalar_prefetch=1,
            grid=(width // COLS,),
            in_specs=[
                pl.BlockSpec((rows, depth), lambda k, at: (0, 0)),
                pl.BlockSpec((depth, COLS), lambda k, at: (0, at[0] + k)),
            ],
            out_specs=pl.BlockSpec((rows, COLS), lambda k, at: (0, k)),
        ),
        out_shape=jax.ShapeDtypeStruct((rows, width), kind),
        compiler_params=pltpu.CompilerParams(vmem_limit_bytes=48 * 2**20),
        cost_estimate=pl.CostEstimate(flops=2 * rows * depth * width, bytes_accessed=depth * width * 2, transcendentals=0),
    )(at.reshape(1), hidden, w)


def on_device(tokens, expert_ids, gate_ranks, limits, w_in, w_out):
    tok_dev = expert_ids.shape[0]
    slot_count = lax.axis_size("expert")
    slices = slot_count // EXP_WIN
    hid_local = w_in.shape[3]
    chosen = expert_ids.reshape(-1)
    labels = jnp.arange(NUM_EXPERTS, dtype=jnp.int32)
    onehot = (chosen[:, None] == labels[None, :]).astype(jnp.int32)
    before = jnp.cumsum(onehot, axis=0) - onehot
    position = jnp.sum(before * onehot, axis=1)
    limit_of = jnp.sum(onehot * limits[0][None, :], axis=1)
    keep_mask = (chosen < EXP_WIN) & (position < limit_of)
    rank_vals = gate_ranks.astype(jnp.float32)
    gate_share = (rank_vals / jnp.sum(rank_vals, axis=1, keepdims=True)).reshape(-1)
    slot_index = chosen * CAP + position
    columns = jnp.arange(EXP_WIN * CAP, dtype=jnp.int32)
    select = (keep_mask[:, None] & (slot_index[:, None] == columns[None, :])).astype(jnp.float32)
    owners = (
        (jnp.arange(tok_dev * 2, dtype=jnp.int32) // 2)[:, None]
        == jnp.arange(tok_dev, dtype=jnp.int32)[None, :]
    ).astype(jnp.float32)
    pick_matrix = jnp.dot(select.T, owners, preferred_element_type=jnp.float32).astype(jnp.bfloat16)
    combine = jnp.dot(
        owners.T,
        select * gate_share[:, None],
        preferred_element_type=jnp.float32,
        precision=lax.Precision.HIGHEST,
    )
    half = tokens.shape[1]
    width = half // CHUNKS
    same_rank = [[e * slices + r for e in range(EXP_WIN)] for r in range(slices)]
    same_expert = [[e * slices + r for r in range(slices)] for e in range(EXP_WIN)]
    core = lax.axis_index("mp")
    weights = w_in[0].reshape(D, 2, hid_local // 128, 128).transpose(0, 2, 1, 3)
    weights = weights.reshape(D, hid_local // 64, 128)

    sums = None
    for c in range(CHUNKS):
        part = tokens[:, c * width:(c + 1) * width]
        outgoing = jnp.dot(pick_matrix, part, preferred_element_type=jnp.float32).astype(jnp.bfloat16)
        outgoing = outgoing.reshape(EXP_WIN, CAP, width)
        arrived = lax.all_to_all(
            outgoing, "expert", split_axis=0, concat_axis=0, axis_index_groups=same_rank, tiled=True
        ).reshape(EXP_WIN * CAP, width)
        pairs = [[2 * i + m for i in group for m in range(2)] for group in same_expert]
        rows = lax.all_gather(arrived, ("expert", "mp"), axis_index_groups=pairs)
        rows = rows.reshape(slices, 2, EXP_WIN * CAP, width)
        sums = gate_up(rows, weights, sums, c, c == CHUNKS - 1)
    hidden = sums

    mixed = []
    for c in range(CHUNKS):
        tiles = half // COLS
        start = c * (width // COLS)
        theirs = down(hidden, w_out[0], (1 - core) * tiles + start, width, jnp.bfloat16)
        landed = lax.ppermute(theirs, "mp", [(0, 1), (1, 0)])
        mine = down(hidden, w_out[0], core * tiles + start, width, jnp.float32)
        share = (mine + landed.astype(jnp.float32)).astype(jnp.bfloat16)
        share = share.reshape(slices, EXP_WIN * CAP, width)
        rank = lax.rem(lax.axis_index("expert"), slices)
        total = lax.dynamic_index_in_dim(share, rank, 0, False).astype(jnp.float32)
        for d in range(1, slices):
            sent = lax.dynamic_index_in_dim(share, lax.rem(rank + d, slices), 0, False)
            ring = [(g[r], g[(r + d) % slices]) for g in same_expert for r in range(slices)]
            total = total + lax.ppermute(sent, "expert", ring).astype(jnp.float32)
        total = total.astype(jnp.bfloat16).reshape(EXP_WIN, CAP, width)
        returned = lax.all_to_all(
            total, "expert", split_axis=0, concat_axis=0, axis_index_groups=same_rank, tiled=True
        ).reshape(EXP_WIN * CAP, width)
        mixed.append(jnp.dot(
            combine,
            returned.astype(jnp.float32),
            preferred_element_type=jnp.float32,
            precision=lax.Precision.HIGHEST,
        ).astype(jnp.bfloat16))
    return jnp.concatenate(mixed, axis=1)


def solution(mesh):
    placed = (
        P(("groups", "expert"), "mp"),
        P(("groups", "expert"), None),
        P(("groups", "expert"), None),
        P(("groups", "expert"), None),
        P("expert", None, None, "mp"),
        P("expert", "mp", None),
    )
    return jax.shard_map(
        on_device,
        mesh=mesh,
        in_specs=placed,
        out_specs=P(("groups", "expert"), "mp"),
        check_vma=False,
    )
```

```python
import functools
import jax
import jax.numpy as jnp
from jax import lax
from jax.experimental import pallas as pl
from jax.experimental.pallas import tpu as pltpu
from jax.sharding import PartitionSpec as P

D = 6144
NUM_EXPERTS = 8
EXP_WIN = 4
CAP = 24

CHUNKS = 3
STEP = 512
COLS = 512


def gate_up_body(steps, first, last, *refs):
    if first:
        _, own_ref, other_ref, w_ref, o_ref, *rest = refs
    else:
        _, own_ref, other_ref, w_ref, before_ref, o_ref, *rest = refs
    sums = rest[0] if last else o_ref
    step = pl.program_id(0)

    @pl.when(step == 0)
    def _():
        sums[...] = jnp.zeros_like(sums) if first else before_ref[...]

    depth = w_ref.shape[0]
    x = jnp.where(step < steps // 2, own_ref[...], other_ref[...])
    w = w_ref[...].reshape(depth, sums.shape[1])
    sums[...] += jnp.dot(x, w, preferred_element_type=jnp.float32)

    if last:
        @pl.when(step == steps - 1)
        def _():
            for j in range(o_ref.shape[1] // 128):
                gate = sums[:, 256 * j:256 * j + 128]
                up = sums[:, 256 * j + 128:256 * j + 256]
                o_ref[:, 128 * j:128 * j + 128] = (gate * jax.nn.sigmoid(gate) * up).astype(o_ref.dtype)


def gate_up(own, other, w, before, at, last):
    rows, width = own.shape
    wide = w.shape[1] * 128
    per_half = width // STEP
    steps = 2 * per_half
    first = before is None
    in_specs = [
        pl.BlockSpec((rows, STEP), lambda k, at: (0, jnp.minimum(k, per_half - 1))),
        pl.BlockSpec((rows, STEP), lambda k, at: (0, jnp.maximum(k - per_half, 0))),
        pl.BlockSpec((STEP, w.shape[1], 128), lambda k, at: (at[k // per_half] + k % per_half, 0, 0)),
    ]
    if not first:
        in_specs.append(pl.BlockSpec((rows, wide), lambda k, at: (0, 0)))
    out = jax.ShapeDtypeStruct((rows, wide // 2), jnp.bfloat16) if last else jax.ShapeDtypeStruct((rows, wide), jnp.float32)
    return pl.pallas_call(
        functools.partial(gate_up_body, steps, first, last),
        grid_spec=pltpu.PrefetchScalarGridSpec(
            num_scalar_prefetch=1,
            grid=(steps,),
            in_specs=in_specs,
            out_specs=pl.BlockSpec(out.shape, lambda k, at: (0, 0)),
            scratch_shapes=[pltpu.VMEM((rows, wide), jnp.float32)] if last else [],
        ),
        out_shape=out,
        compiler_params=pltpu.CompilerParams(vmem_limit_bytes=48 * 2**20),
        cost_estimate=pl.CostEstimate(flops=4 * rows * width * wide, bytes_accessed=4 * width * wide, transcendentals=0),
    )(*([at, own, other, w] if first else [at, own, other, w, before]))


def down_body(at_ref, h_ref, w_ref, o_ref):
    o_ref[...] = jnp.dot(h_ref[...], w_ref[...], preferred_element_type=jnp.float32).astype(o_ref.dtype)


def down(hidden, w, at, width, kind):
    rows, depth = hidden.shape
    return pl.pallas_call(
        down_body,
        grid_spec=pltpu.PrefetchScalarGridSpec(
            num_scalar_prefetch=1,
            grid=(width // COLS,),
            in_specs=[
                pl.BlockSpec((rows, depth), lambda k, at: (0, 0)),
                pl.BlockSpec((depth, COLS), lambda k, at: (0, at[0] + k)),
            ],
            out_specs=pl.BlockSpec((rows, COLS), lambda k, at: (0, k)),
        ),
        out_shape=jax.ShapeDtypeStruct((rows, width), kind),
        compiler_params=pltpu.CompilerParams(vmem_limit_bytes=48 * 2**20),
        cost_estimate=pl.CostEstimate(flops=2 * rows * depth * width, bytes_accessed=depth * width * 2, transcendentals=0),
    )(at.reshape(1), hidden, w)


def on_device(tokens, expert_ids, gate_ranks, limits, w_in, w_out):
    tok_dev = expert_ids.shape[0]
    slot_count = lax.axis_size("expert")
    slices = slot_count // EXP_WIN
    hid_local = w_in.shape[3]
    chosen = expert_ids.reshape(-1)
    labels = jnp.arange(NUM_EXPERTS, dtype=jnp.int32)
    onehot = (chosen[:, None] == labels[None, :]).astype(jnp.int32)
    before = jnp.cumsum(onehot, axis=0) - onehot
    position = jnp.sum(before * onehot, axis=1)
    limit_of = jnp.sum(onehot * limits[0][None, :], axis=1)
    keep_mask = (chosen < EXP_WIN) & (position < limit_of)
    rank_vals = gate_ranks.astype(jnp.float32)
    gate_share = (rank_vals / jnp.sum(rank_vals, axis=1, keepdims=True)).reshape(-1)
    turned = lax.rem(chosen - lax.axis_index("expert") // slices + NUM_EXPERTS, EXP_WIN)
    slot_index = turned * CAP + position
    columns = jnp.arange(EXP_WIN * CAP, dtype=jnp.int32)
    select = (keep_mask[:, None] & (slot_index[:, None] == columns[None, :])).astype(jnp.float32)
    owners = (
        (jnp.arange(tok_dev * 2, dtype=jnp.int32) // 2)[:, None]
        == jnp.arange(tok_dev, dtype=jnp.int32)[None, :]
    ).astype(jnp.float32)
    pick_matrix = jnp.dot(select.T, owners, preferred_element_type=jnp.float32).astype(jnp.bfloat16)
    combine = jnp.dot(
        owners.T,
        select * gate_share[:, None],
        preferred_element_type=jnp.float32,
        precision=lax.Precision.HIGHEST,
    )
    half = tokens.shape[1]
    width = half // CHUNKS
    core = lax.axis_index("mp")
    spots = [(e, r) for e in range(EXP_WIN) for r in range(slices)]

    def to_expert(x, d):
        return lax.ppermute(x, "expert", [(e * slices + r, (e + d) % EXP_WIN * slices + r) for e, r in spots])

    def to_rank(x, d):
        return lax.ppermute(x, "expert", [(e * slices + r, e * slices + (r + d) % slices) for e, r in spots])

    def to_core(x):
        return lax.ppermute(x, "mp", [(0, 1), (1, 0)])

    weights = w_in[0].reshape(D, 2, hid_local // 128, 128).transpose(0, 2, 1, 3)
    weights = weights.reshape(D, hid_local // 64, 128)
    outgoing = jnp.dot(pick_matrix, tokens, preferred_element_type=jnp.float32).astype(jnp.bfloat16)

    sums = None
    for c in range(CHUNKS):
        part = outgoing[:, c * width:(c + 1) * width].reshape(EXP_WIN, CAP, width)
        arrived = jnp.concatenate([part[0]] + [to_expert(part[d], d) for d in range(1, EXP_WIN)], axis=0)
        own = jnp.concatenate([arrived] + [to_rank(arrived, d) for d in range(1, slices)], axis=0)
        other = to_core(own)
        at = (jnp.stack([core, 1 - core]) * half + c * width) // STEP
        sums = gate_up(own, other, weights, sums, at.astype(jnp.int32), c == CHUNKS - 1)
    hidden = sums

    mixed = []
    for c in range(CHUNKS):
        tiles = half // COLS
        start = c * (width // COLS)
        theirs = down(hidden, w_out[0], (1 - core) * tiles + start, width, jnp.bfloat16)
        landed = to_core(theirs)
        mine = down(hidden, w_out[0], core * tiles + start, width, jnp.float32)
        share = (mine + landed.astype(jnp.float32)).astype(jnp.bfloat16)
        share = share.reshape(slices, EXP_WIN * CAP, width)
        total = share[0].astype(jnp.float32)
        for d in range(1, slices):
            total = total + to_rank(share[d], slices - d).astype(jnp.float32)
        total = total.astype(jnp.bfloat16).reshape(EXP_WIN, CAP, width)
        returned = jnp.concatenate([total[0]] + [to_expert(total[d], EXP_WIN - d) for d in range(1, EXP_WIN)], axis=0)
        mixed.append(jnp.dot(
            combine,
            returned.astype(jnp.float32),
            preferred_element_type=jnp.float32,
            precision=lax.Precision.HIGHEST,
        ).astype(jnp.bfloat16))
    return jnp.concatenate(mixed, axis=1)


def solution(mesh):
    placed = (
        P(("groups", "expert"), "mp"),
        P(("groups", "expert"), None),
        P(("groups", "expert"), None),
        P(("groups", "expert"), None),
        P("expert", None, None, "mp"),
        P("expert", "mp", None),
    )
    return jax.shard_map(
        on_device,
        mesh=mesh,
        in_specs=placed,
        out_specs=P(("groups", "expert"), "mp"),
        check_vma=False,
    )
```

```python
import functools
import jax
import jax.numpy as jnp
from jax import lax
from jax.experimental import pallas as pl
from jax.experimental.pallas import tpu as pltpu
from jax.sharding import PartitionSpec as P

D = 6144
NUM_EXPERTS = 8
EXP_WIN = 4
CAP = 24

CHUNKS = 3
STEP = 512
COLS = 512


def gate_up_body(steps, first, last, *refs):
    if first:
        _, own_ref, other_ref, w_ref, o_ref, *rest = refs
    else:
        _, own_ref, other_ref, w_ref, before_ref, o_ref, *rest = refs
    sums = rest[0] if last else o_ref
    step = pl.program_id(0)

    @pl.when(step == 0)
    def _():
        sums[...] = jnp.zeros_like(sums) if first else before_ref[...]

    depth = w_ref.shape[0]
    x = jnp.where(step < steps // 2, own_ref[...], other_ref[...])
    w = w_ref[...].reshape(depth, sums.shape[1])
    sums[...] += jnp.dot(x, w, preferred_element_type=jnp.float32)

    if last:
        @pl.when(step == steps - 1)
        def _():
            for j in range(o_ref.shape[1] // 128):
                gate = sums[:, 256 * j:256 * j + 128]
                up = sums[:, 256 * j + 128:256 * j + 256]
                o_ref[:, 128 * j:128 * j + 128] = (gate * jax.nn.sigmoid(gate) * up).astype(o_ref.dtype)


def gate_up(own, other, w, before, at, last):
    rows, width = own.shape
    wide = w.shape[1] * 128
    per_half = width // STEP
    steps = 2 * per_half
    first = before is None
    in_specs = [
        pl.BlockSpec((rows, STEP), lambda k, at: (0, jnp.minimum(k, per_half - 1))),
        pl.BlockSpec((rows, STEP), lambda k, at: (0, jnp.maximum(k - per_half, 0))),
        pl.BlockSpec((STEP, w.shape[1], 128), lambda k, at: (at[k // per_half] + k % per_half, 0, 0)),
    ]
    if not first:
        in_specs.append(pl.BlockSpec((rows, wide), lambda k, at: (0, 0)))
    out = jax.ShapeDtypeStruct((rows, wide // 2), jnp.bfloat16) if last else jax.ShapeDtypeStruct((rows, wide), jnp.float32)
    return pl.pallas_call(
        functools.partial(gate_up_body, steps, first, last),
        grid_spec=pltpu.PrefetchScalarGridSpec(
            num_scalar_prefetch=1,
            grid=(steps,),
            in_specs=in_specs,
            out_specs=pl.BlockSpec(out.shape, lambda k, at: (0, 0)),
            scratch_shapes=[pltpu.VMEM((rows, wide), jnp.float32)] if last else [],
        ),
        out_shape=out,
        compiler_params=pltpu.CompilerParams(vmem_limit_bytes=48 * 2**20),
        cost_estimate=pl.CostEstimate(flops=4 * rows * width * wide, bytes_accessed=4 * width * wide, transcendentals=0),
    )(*([at, own, other, w] if first else [at, own, other, w, before]))


def down_body(at_ref, h_ref, w_ref, o_ref):
    o_ref[...] = jnp.dot(h_ref[...], w_ref[...], preferred_element_type=jnp.float32).astype(o_ref.dtype)


def down(hidden, w, at, width, kind):
    rows, depth = hidden.shape
    return pl.pallas_call(
        down_body,
        grid_spec=pltpu.PrefetchScalarGridSpec(
            num_scalar_prefetch=1,
            grid=(width // COLS,),
            in_specs=[
                pl.BlockSpec((rows, depth), lambda k, at: (0, 0)),
                pl.BlockSpec((depth, COLS), lambda k, at: (0, at[0] + k)),
            ],
            out_specs=pl.BlockSpec((rows, COLS), lambda k, at: (0, k)),
        ),
        out_shape=jax.ShapeDtypeStruct((rows, width), kind),
        compiler_params=pltpu.CompilerParams(vmem_limit_bytes=48 * 2**20),
        cost_estimate=pl.CostEstimate(flops=2 * rows * depth * width, bytes_accessed=depth * width * 2, transcendentals=0),
    )(at.reshape(1), hidden, w)


def on_device(tokens, expert_ids, gate_ranks, limits, w_in, w_out):
    tok_dev = expert_ids.shape[0]
    slot_count = lax.axis_size("expert")
    slices = slot_count // EXP_WIN
    hid_local = w_in.shape[3]
    chosen = expert_ids.reshape(-1)
    labels = jnp.arange(NUM_EXPERTS, dtype=jnp.int32)
    onehot = (chosen[:, None] == labels[None, :]).astype(jnp.int32)
    before = jnp.cumsum(onehot, axis=0) - onehot
    position = jnp.sum(before * onehot, axis=1)
    limit_of = jnp.sum(onehot * limits[0][None, :], axis=1)
    keep_mask = (chosen < EXP_WIN) & (position < limit_of)
    rank_vals = gate_ranks.astype(jnp.float32)
    gate_share = (rank_vals / jnp.sum(rank_vals, axis=1, keepdims=True)).reshape(-1)
    turned = lax.rem(chosen - lax.axis_index("expert") // slices + NUM_EXPERTS, EXP_WIN)
    slot_index = turned * CAP + position
    columns = jnp.arange(EXP_WIN * CAP, dtype=jnp.int32)
    select = (keep_mask[:, None] & (slot_index[:, None] == columns[None, :])).astype(jnp.float32)
    owners = (
        (jnp.arange(tok_dev * 2, dtype=jnp.int32) // 2)[:, None]
        == jnp.arange(tok_dev, dtype=jnp.int32)[None, :]
    ).astype(jnp.float32)
    pick_matrix = jnp.dot(select.T, owners, preferred_element_type=jnp.float32).astype(jnp.bfloat16)
    combine = jnp.dot(
        owners.T,
        select * gate_share[:, None],
        preferred_element_type=jnp.float32,
        precision=lax.Precision.HIGHEST,
    )
    half = tokens.shape[1]
    width = half // CHUNKS
    core = lax.axis_index("mp")
    spots = [(e, r) for e in range(EXP_WIN) for r in range(slices)]

    def to_expert(x, d):
        return lax.ppermute(x, "expert", [(e * slices + r, (e + d) % EXP_WIN * slices + r) for e, r in spots])

    def to_rank(x, d):
        return lax.ppermute(x, "expert", [(e * slices + r, e * slices + (r + d) % slices) for e, r in spots])

    def to_core(x):
        return lax.ppermute(x, "mp", [(0, 1), (1, 0)])

    weights = w_in[0].reshape(D, 2, hid_local // 128, 128).transpose(0, 2, 1, 3)
    weights = weights.reshape(D, hid_local // 64, 128)
    outgoing = jnp.dot(pick_matrix, tokens, preferred_element_type=jnp.float32).astype(jnp.bfloat16)

    def after(x, *others):
        return lax.optimization_barrier((x,) + others)[0]

    arrived, own = [], []
    for c in range(CHUNKS):
        part = outgoing[:, c * width:(c + 1) * width].reshape(EXP_WIN, CAP, width)
        arrived.append(jnp.concatenate([part[0]] + [to_expert(part[d], d) for d in range(1, EXP_WIN)], axis=0))
        own.append(jnp.concatenate([arrived[c]] + [to_rank(arrived[c], d) for d in range(1, slices)], axis=0))

    sums = []
    for c in range(CHUNKS):
        other = to_core(own[c] if c < 2 else after(own[c], sums[c - 2]))
        waits = own[c + 1:c + 2] + arrived[c + 2:c + 3]
        if waits:
            other = after(other, *waits)
        at = (jnp.stack([core, 1 - core]) * half + c * width) // STEP
        before = sums[c - 1] if c else None
        sums.append(gate_up(own[c], other, weights, before, at.astype(jnp.int32), c == CHUNKS - 1))
    hidden = sums[-1]

    mixed, shares, totals = [], [], []
    for c in range(CHUNKS):
        tiles = half // COLS
        start = c * (width // COLS)
        if c:
            hidden = after(hidden, shares[c - 1], *totals[:c - 1])
        theirs = down(hidden, w_out[0], (1 - core) * tiles + start, width, jnp.bfloat16)
        landed = to_core(theirs)
        mine = down(after(hidden, theirs), w_out[0], core * tiles + start, width, jnp.float32)
        share = (mine + landed.astype(jnp.float32)).astype(jnp.bfloat16)
        shares.append(share)
        share = share.reshape(slices, EXP_WIN * CAP, width)
        total = share[0].astype(jnp.float32)
        for d in range(1, slices):
            total = total + to_rank(share[d], slices - d).astype(jnp.float32)
        total = total.astype(jnp.bfloat16)
        totals.append(total)
        total = total.reshape(EXP_WIN, CAP, width)
        returned = jnp.concatenate([total[0]] + [to_expert(total[d], EXP_WIN - d) for d in range(1, EXP_WIN)], axis=0)
        mixed.append(jnp.dot(
            combine,
            returned.astype(jnp.float32),
            preferred_element_type=jnp.float32,
            precision=lax.Precision.HIGHEST,
        ).astype(jnp.bfloat16))
    return jnp.concatenate(mixed, axis=1)


def solution(mesh):
    placed = (
        P(("groups", "expert"), "mp"),
        P(("groups", "expert"), None),
        P(("groups", "expert"), None),
        P(("groups", "expert"), None),
        P("expert", None, None, "mp"),
        P("expert", "mp", None),
    )
    return jax.shard_map(
        on_device,
        mesh=mesh,
        in_specs=placed,
        out_specs=P(("groups", "expert"), "mp"),
        check_vma=False,
    )
```

```python
import functools
import jax
import jax.numpy as jnp
from jax import lax
from jax.experimental import pallas as pl
from jax.experimental.pallas import tpu as pltpu
from jax.sharding import PartitionSpec as P

D = 6144
NUM_EXPERTS = 8
EXP_WIN = 4
CAP = 24

CHUNKS = 2
STEP = 512
COLS = 512


def gate_up_body(steps, first, last, *refs):
    if first:
        _, own_ref, other_ref, w_ref, o_ref, *rest = refs
    else:
        _, own_ref, other_ref, w_ref, before_ref, o_ref, *rest = refs
    sums = rest[0] if last else o_ref
    step = pl.program_id(0)

    @pl.when(step == 0)
    def _():
        sums[...] = jnp.zeros_like(sums) if first else before_ref[...]

    depth = w_ref.shape[0]
    x = jnp.where(step < steps // 2, own_ref[...], other_ref[...])
    w = w_ref[...].reshape(depth, sums.shape[1])
    sums[...] += jnp.dot(x, w, preferred_element_type=jnp.float32)

    if last:
        @pl.when(step == steps - 1)
        def _():
            for j in range(o_ref.shape[1] // 128):
                gate = sums[:, 256 * j:256 * j + 128]
                up = sums[:, 256 * j + 128:256 * j + 256]
                o_ref[:, 128 * j:128 * j + 128] = (gate * jax.nn.sigmoid(gate) * up).astype(o_ref.dtype)


def gate_up(own, other, w, before, at, last):
    rows, width = own.shape
    wide = w.shape[1] * 128
    per_half = width // STEP
    steps = 2 * per_half
    first = before is None
    in_specs = [
        pl.BlockSpec((rows, STEP), lambda k, at: (0, jnp.minimum(k, per_half - 1))),
        pl.BlockSpec((rows, STEP), lambda k, at: (0, jnp.maximum(k - per_half, 0))),
        pl.BlockSpec((STEP, w.shape[1], 128), lambda k, at: (at[k // per_half] + k % per_half, 0, 0)),
    ]
    if not first:
        in_specs.append(pl.BlockSpec((rows, wide), lambda k, at: (0, 0)))
    out = jax.ShapeDtypeStruct((rows, wide // 2), jnp.bfloat16) if last else jax.ShapeDtypeStruct((rows, wide), jnp.float32)
    return pl.pallas_call(
        functools.partial(gate_up_body, steps, first, last),
        grid_spec=pltpu.PrefetchScalarGridSpec(
            num_scalar_prefetch=1,
            grid=(steps,),
            in_specs=in_specs,
            out_specs=pl.BlockSpec(out.shape, lambda k, at: (0, 0)),
            scratch_shapes=[pltpu.VMEM((rows, wide), jnp.float32)] if last else [],
        ),
        out_shape=out,
        compiler_params=pltpu.CompilerParams(vmem_limit_bytes=48 * 2**20),
        cost_estimate=pl.CostEstimate(flops=4 * rows * width * wide, bytes_accessed=4 * width * wide, transcendentals=0),
    )(*([at, own, other, w] if first else [at, own, other, w, before]))


def down_body(at_ref, h_ref, w_ref, o_ref):
    o_ref[...] = jnp.dot(h_ref[...], w_ref[...], preferred_element_type=jnp.float32).astype(o_ref.dtype)


def down(hidden, w, at, width, kind):
    rows, depth = hidden.shape
    return pl.pallas_call(
        down_body,
        grid_spec=pltpu.PrefetchScalarGridSpec(
            num_scalar_prefetch=1,
            grid=(width // COLS,),
            in_specs=[
                pl.BlockSpec((rows, depth), lambda k, at: (0, 0)),
                pl.BlockSpec((depth, COLS), lambda k, at: (0, at[0] + k)),
            ],
            out_specs=pl.BlockSpec((rows, COLS), lambda k, at: (0, k)),
        ),
        out_shape=jax.ShapeDtypeStruct((rows, width), kind),
        compiler_params=pltpu.CompilerParams(vmem_limit_bytes=48 * 2**20),
        cost_estimate=pl.CostEstimate(flops=2 * rows * depth * width, bytes_accessed=depth * width * 2, transcendentals=0),
    )(at.reshape(1), hidden, w)


def on_device(tokens, expert_ids, gate_ranks, limits, w_in, w_out):
    tok_dev = expert_ids.shape[0]
    slot_count = lax.axis_size("expert")
    slices = slot_count // EXP_WIN
    hid_local = w_in.shape[3]
    chosen = expert_ids.reshape(-1)
    labels = jnp.arange(NUM_EXPERTS, dtype=jnp.int32)
    onehot = (chosen[:, None] == labels[None, :]).astype(jnp.int32)
    before = jnp.cumsum(onehot, axis=0) - onehot
    position = jnp.sum(before * onehot, axis=1)
    limit_of = jnp.sum(onehot * limits[0][None, :], axis=1)
    keep_mask = (chosen < EXP_WIN) & (position < limit_of)
    rank_vals = gate_ranks.astype(jnp.float32)
    gate_share = (rank_vals / jnp.sum(rank_vals, axis=1, keepdims=True)).reshape(-1)
    turned = lax.rem(chosen - lax.axis_index("expert") // slices + NUM_EXPERTS, EXP_WIN)
    slot_index = turned * CAP + position
    columns = jnp.arange(EXP_WIN * CAP, dtype=jnp.int32)
    select = (keep_mask[:, None] & (slot_index[:, None] == columns[None, :])).astype(jnp.float32)
    owners = (
        (jnp.arange(tok_dev * 2, dtype=jnp.int32) // 2)[:, None]
        == jnp.arange(tok_dev, dtype=jnp.int32)[None, :]
    ).astype(jnp.float32)
    pick_matrix = jnp.dot(select.T, owners, preferred_element_type=jnp.float32).astype(jnp.bfloat16)
    combine = jnp.dot(
        owners.T,
        select * gate_share[:, None],
        preferred_element_type=jnp.float32,
        precision=lax.Precision.HIGHEST,
    )
    half = tokens.shape[1]
    width = half // CHUNKS
    core = lax.axis_index("mp")
    spots = [(e, r) for e in range(EXP_WIN) for r in range(slices)]

    def to_expert(x, d):
        return lax.ppermute(x, "expert", [(e * slices + r, (e + d) % EXP_WIN * slices + r) for e, r in spots])

    def to_rank(x, d):
        return lax.ppermute(x, "expert", [(e * slices + r, e * slices + (r + d) % slices) for e, r in spots])

    def to_core(x):
        return lax.ppermute(x, "mp", [(0, 1), (1, 0)])

    weights = w_in[0].reshape(D, 2, hid_local // 128, 128).transpose(0, 2, 1, 3)
    weights = weights.reshape(D, hid_local // 64, 128)
    outgoing = jnp.dot(pick_matrix, tokens, preferred_element_type=jnp.float32).astype(jnp.bfloat16)

    def after(x, *others):
        return lax.optimization_barrier((x,) + others)[0]

    arrived, own = [], []
    for c in range(CHUNKS):
        part = outgoing[:, c * width:(c + 1) * width].reshape(EXP_WIN, CAP, width)
        arrived.append(jnp.concatenate([part[0]] + [to_expert(part[d], d) for d in range(1, EXP_WIN)], axis=0))
        own.append(jnp.concatenate([arrived[c]] + [to_rank(arrived[c], d) for d in range(1, slices)], axis=0))

    sums = []
    for c in range(CHUNKS):
        other = to_core(own[c] if c < 2 else after(own[c], sums[c - 2]))
        waits = own[c + 1:c + 2] + arrived[c + 2:c + 3]
        if waits:
            other = after(other, *waits)
        at = (jnp.stack([core, 1 - core]) * half + c * width) // STEP
        before = sums[c - 1] if c else None
        sums.append(gate_up(own[c], other, weights, before, at.astype(jnp.int32), c == CHUNKS - 1))
    hidden = sums[-1]

    mixed, shares, totals = [], [], []
    for c in range(CHUNKS):
        tiles = half // COLS
        start = c * (width // COLS)
        if c:
            hidden = after(hidden, shares[c - 1], *totals[:c - 1])
        theirs = down(hidden, w_out[0], (1 - core) * tiles + start, width, jnp.bfloat16)
        landed = to_core(theirs)
        mine = down(after(hidden, theirs), w_out[0], core * tiles + start, width, jnp.float32)
        share = (mine + landed.astype(jnp.float32)).astype(jnp.bfloat16)
        shares.append(share)
        share = share.reshape(slices, EXP_WIN * CAP, width)
        total = share[0].astype(jnp.float32)
        for d in range(1, slices):
            total = total + to_rank(share[d], slices - d).astype(jnp.float32)
        total = total.astype(jnp.bfloat16)
        totals.append(total)
        total = total.reshape(EXP_WIN, CAP, width)
        returned = jnp.concatenate([total[0]] + [to_expert(total[d], EXP_WIN - d) for d in range(1, EXP_WIN)], axis=0)
        mixed.append(jnp.dot(
            combine,
            returned.astype(jnp.float32),
            preferred_element_type=jnp.float32,
            precision=lax.Precision.HIGHEST,
        ).astype(jnp.bfloat16))
    return jnp.concatenate(mixed, axis=1)


def solution(mesh):
    placed = (
        P(("groups", "expert"), "mp"),
        P(("groups", "expert"), None),
        P(("groups", "expert"), None),
        P(("groups", "expert"), None),
        P("expert", None, None, "mp"),
        P("expert", "mp", None),
    )
    return jax.shard_map(
        on_device,
        mesh=mesh,
        in_specs=placed,
        out_specs=P(("groups", "expert"), "mp"),
        check_vma=False,
    )
```
